256 devices in a mesh: section: 2 (over core), tile: 32 (over y, z), wave: 4 (over x).
Axes of the slice: x: 4, y: 4, z: 8, core: 2. Of those that a mesh axis runs over, the one named last changes fastest.
Arguments:
- rf_rows: bfloat16 [8, 64, 1024, 2048], P('wave', None, ('section', 'tile')), may hold values from -14 to 14
- filter_taps: bfloat16 [128], replicated, may hold values from -0.5 to 0.5
- interp_weights: bfloat16 [64, 16, 2048, 128], P(('section', 'tile')), may hold values from -0.125 to 0.125
- apodization: float32 [8, 32, 128], P('wave'), may hold values from 0.1 to 1
- fanout: int32 [64, 16], P(('section', 'tile')), may hold values from 0 to 31, as said below
- live_slots: int32 [64], P(('section', 'tile')), may hold values from 1 to 16, as said below
- offsets: int32 [64, 16, 8], P(('section', 'tile'), None, 'wave'), may hold values from 128 to 1920
- owned_tiles: int32 [32], replicated, may hold values from 0 to 31, each once
Outputs:
- doppler: float32 [32, 128], P('tile')
The draws below stay inside these ranges and needn't reach their ends.
Inputs may be any that keep to these rules, and one draw needn't show every extreme that they name: `fanout`: each row names 16 different voxel tiles; row b begins with b % 32. Element tile b feeds the voxel tiles of the first live_slots[b] entries of its fanout row; later entries are unused. Some element tile has all 16 live.
All inputs are finite; a program needn't handle non-finite values.
Results may differ from the reference program's by a relative error of at most 0.0022.
Values sent between devices are 32-bit elements; how exact they have to be, the bound alone decides.
No kernel may reach another device: no remote copies, remote signals or barrier semaphores. Data moves between devices by JAX's collectives and lax.ppermute only.
A program may use at most 64 MiB of HBM per device.

```python
import math
import jax
import jax.numpy as jnp
from jax import lax

ELEMENTS = 1024
SAMPLES = 2048
TAPS = 128
SEG = 128
VOX_TILE = 128
FRAMES = 64
WAVES = 8
ETILES = 64
TILE_ELEMS = 16
FAN = 16
N_TILE = 32


def draw_rf_rows(key, part):
    key = jax.random.fold_in(key, 11)
    key_common, key_fresh = jax.random.split(key)
    common = jax.random.normal(key_common, (WAVES, 1, ELEMENTS, SAMPLES), jnp.float32)
    fresh_part = jax.random.normal(key_fresh, (WAVES, FRAMES, ELEMENTS, SAMPLES), jnp.float32)
    combined = 2.0 * common + fresh_part
    return jnp.clip(combined, -14.0, 14.0).astype(jnp.bfloat16)


def draw_fanout(key, part):
    key = jax.random.fold_in(key, 5)
    streams = jax.random.split(key, ETILES)
    shuffled = jax.vmap(lambda stream: jax.random.permutation(stream, N_TILE - 1))(streams) + 1
    rotation = jnp.concatenate([jnp.zeros((ETILES, 1), jnp.int32), shuffled.astype(jnp.int32)], axis=1)[:, :FAN]
    anchor = jnp.arange(ETILES, dtype=jnp.int32) % N_TILE
    return ((anchor[:, None] + rotation) % N_TILE).astype(jnp.int32)


def draw_live_slots(key, part):
    key = jax.random.fold_in(key, 7)
    key_loads, key_full = jax.random.split(key)
    live_loads = jax.random.randint(key_loads, (ETILES,), 1, FAN + 1)
    busiest = jax.random.randint(key_full, (), 0, ETILES)
    return jnp.where(jnp.arange(ETILES) == busiest, FAN, jnp.minimum(live_loads, FAN)).astype(jnp.int32)


def touch_ends(entries, rng, least, top_value):
    spot = [jax.random.randint(jax.random.fold_in(rng, axis), (), 0, length) for axis, length in enumerate(entries.shape)]
    widest = entries.shape.index(max(entries.shape))
    next_to = spot[:widest] + [(spot[widest] + 1) % entries.shape[widest]] + spot[widest + 1:]
    return entries.at[tuple(spot)].set(least).at[tuple(next_to)].set(top_value)


def level_of(rng, shape, cuts, least, top_value):
    loudness, own = 1.0, jax.random.fold_in(rng, 6)
    for axis_at, blocks in cuts:
        draws = jnp.exp(jax.random.uniform(jax.random.fold_in(own, axis_at), (blocks,), jnp.float32, least / len(cuts), top_value / len(cuts)))
        loudness = loudness * jnp.repeat(draws, shape[axis_at] // blocks).reshape([-1 if axis == axis_at else 1 for axis in range(len(shape))])
    return loudness


def normal_values(own_key, extent, spread, most, cuts=(), kind=jnp.bfloat16):
    values = spread * jax.random.normal(own_key, extent, jnp.float32)
    if cuts:
        values = values * level_of(own_key, extent, cuts, -0.22, 0.18)
    return jnp.clip(values, -most, most).astype(kind)


def setup_inputs(seed: int = 0) -> dict:
    key_list = jax.random.split(jax.random.key(seed), 9)
    rf_rows = draw_rf_rows(jax.random.fold_in(key_list[8], 71), 0)
    filter_taps = normal_values(key_list[1], (TAPS,), TAPS ** -0.5, 0.5)
    interp_weights = normal_values(key_list[2], (ETILES, FAN, TILE_ELEMS * SEG, VOX_TILE), (TILE_ELEMS * SEG) ** -0.5, 0.125, ((0, 64),))
    apodization = jnp.clip(jnp.exp(math.log(1.0) - 2.3025851 * jax.random.uniform(key_list[3], (WAVES, N_TILE, VOX_TILE), jnp.float32) ** level_of(key_list[3], (WAVES, N_TILE, VOX_TILE), ((0, 4),), -0.2, 0.2)), 0.1, 1.0)
    fanout = draw_fanout(jax.random.fold_in(key_list[8], 71), 0)
    live_slots = draw_live_slots(jax.random.fold_in(key_list[8], 71), 0)
    offsets = touch_ends(jax.random.randint(key_list[6], (ETILES, FAN, WAVES), TAPS, SAMPLES - SEG + 1), jax.random.fold_in(key_list[6], 1), TAPS, SAMPLES - SEG).astype(jnp.int32)
    owned_tiles = jax.random.permutation(key_list[7], N_TILE).astype(jnp.int32)
    return dict(rf_rows=rf_rows, filter_taps=filter_taps, interp_weights=interp_weights, apodization=apodization, fanout=fanout, live_slots=live_slots, offsets=offsets, owned_tiles=owned_tiles)


def toeplitz_table(filter_taps, window, history):
    width = 2 * window + history
    padded = jnp.concatenate([jnp.zeros((width - history,), filter_taps.dtype), filter_taps])
    height = window + history
    flat = jnp.tile(padded, height)[: height * (width - 1)]
    return flat.reshape(height, width - 1)[:, :window]


def reference(rf_rows, filter_taps, interp_weights, apodization, fanout, live_slots, offsets, owned_tiles):
    toeplitz = toeplitz_table(filter_taps, SEG, TAPS).astype(jnp.float32)
    image_start = jnp.zeros((N_TILE, FRAMES, VOX_TILE), jnp.float32)

    def tile_step(image_sum, tile_index):
        first_elem = (tile_index * TILE_ELEMS).astype(jnp.int32)
        elements = lax.dynamic_slice_in_dim(rf_rows, first_elem, TILE_ELEMS, 2)

        def slot_step(slot_index, image_acc):
            starts = (offsets[tile_index, slot_index] - TAPS).astype(jnp.int32)

            def window_cut(wave_rows, wave_start):
                return lax.dynamic_slice_in_dim(wave_rows, wave_start, SEG + TAPS, 2)

            segments = jax.vmap(window_cut)(elements, starts)
            filtered = jnp.einsum("wfet,ts->wfes", segments.astype(jnp.float32), toeplitz).astype(jnp.bfloat16)
            beam = jnp.dot(filtered.reshape(WAVES * FRAMES, TILE_ELEMS * SEG), interp_weights[tile_index, slot_index],
                           preferred_element_type=jnp.float32).reshape(WAVES, FRAMES, VOX_TILE)
            voxel_tile = fanout[tile_index, slot_index].astype(jnp.int32)
            wave_weights = lax.dynamic_index_in_dim(apodization, voxel_tile, 1, keepdims=False)
            term = jnp.sum(wave_weights[:, None, :] * beam, axis=0)
            current = lax.dynamic_index_in_dim(image_acc, voxel_tile, 0, keepdims=False)
            return lax.dynamic_update_index_in_dim(image_acc, current + term, voxel_tile, 0)

        image_sum = lax.fori_loop(0, live_slots[tile_index], slot_step, image_sum)
        return image_sum, tile_index

    image_sum, visited = lax.scan(tile_step, image_start, jnp.arange(ETILES, dtype=jnp.int32))
    clutter = jnp.mean(image_sum, axis=1, keepdims=True)
    deviation = image_sum - clutter
    doppler = jnp.mean(deviation * deviation, axis=1)
    return doppler[owned_tiles]
```

```python
import functools

import jax
import jax.numpy as jnp
from jax import lax
from jax.experimental import pallas as pl
from jax.experimental.pallas import tpu as pltpu
from jax.sharding import PartitionSpec as P

LANES = 128


def beam_kernel(
    side, offsets, fanout, live, owned,
    rf, taps, weights, apod,
    keep, send,
    table, shifted, filtered, place,
):
    slot = pl.program_id(0)
    waves, frames, elems, samples = rf.shape
    window = weights.shape[1] // elems
    history = taps.shape[1]
    reach = window + history + LANES
    half = frames // 2
    tiles = owned.shape[0]

    @pl.when(slot == 0)
    def _():
        keep[...] = jnp.zeros_like(keep)
        send[...] = jnp.zeros_like(send)
        shifted[...] = jnp.zeros_like(shifted)
        rows = table.shape[0]
        line = jnp.concatenate(
            [
                jnp.zeros((1, window + history), jnp.float32),
                taps[...].astype(jnp.float32),
                jnp.zeros((1, rows - window - 2 * history), jnp.float32),
            ],
            axis=1,
        )
        spread = jnp.broadcast_to(line, (rows, rows))
        table[...] = pltpu.roll(spread, 0, 1, stride=1, stride_axis=0)[:, :window]

        def note(index, carry):
            place[owned[index]] = index
            return carry

        lax.fori_loop(0, tiles, note, 0)

    @pl.when(slot < live[0])
    def _():
        bases = []
        for wave in range(waves):
            start = offsets[0, slot, wave] - history
            base = jnp.minimum(start // LANES * LANES, samples - reach)
            shift = start - base
            shifted[
                wave * reach : (wave + 1) * reach, wave * window : (wave + 1) * window
            ] = table[pl.ds(LANES - shift, reach), :].astype(jnp.bfloat16)
            bases.append(pl.multiple_of(base, LANES))
        step = 16
        for first in range(0, frames, step):
            cut = jnp.concatenate(
                [
                    rf[wave, first : first + step, :, pl.ds(bases[wave], reach)].reshape(
                        step * elems, reach
                    )
                    for wave in range(waves)
                ],
                axis=1,
            )
            both = jnp.dot(cut, shifted[...], preferred_element_type=jnp.float32)
            for wave in range(waves):
                filtered[wave, first * elems : (first + step) * elems, :] = both[
                    :, wave * window : (wave + 1) * window
                ]
        beam = jnp.zeros((waves * frames, weights.shape[2]), jnp.float32)
        for elem in range(0, elems, 2):
            columns = []
            for each in (elem, elem + 1):
                columns.append(
                    jnp.concatenate(
                        [
                            filtered[w, pl.ds(each, frames, stride=elems), :].astype(jnp.bfloat16)
                            for w in range(waves)
                        ],
                        axis=0,
                    )
                )
            beam += jnp.dot(
                jnp.concatenate(columns, axis=1),
                weights[0, elem * window : (elem + 2) * window, :],
                preferred_element_type=jnp.float32,
            )
        voxel_tile = fanout[0, slot]
        term = jnp.zeros((frames, weights.shape[2]), jnp.float32)
        for wave in range(waves):
            term += apod[wave, pl.ds(voxel_tile, 1), :] * beam[wave * frames : (wave + 1) * frames]
        term -= jnp.sum(term, axis=0, keepdims=True) * (1.0 / frames)
        where = place[voxel_tile]
        swap = side[0] == 1
        keep[where] = jnp.where(swap, term[half:], term[:half])
        send[where] = jnp.where(swap, term[:half], term[half:])


def local_images(side, rf, taps, weights, apod, fanout, live, offsets, owned):
    waves, frames, elems, samples = rf.shape
    slots, depth, voxels = weights.shape[1:]
    window = depth // elems
    history = taps.shape[0]
    reach = window + history + LANES
    tiles = owned.shape[0]
    image = jax.ShapeDtypeStruct((tiles, frames // 2, voxels), jnp.float32)

    def whole(shape):
        return pl.BlockSpec(shape, lambda i, *_: (0,) * len(shape), pipeline_mode=pl.Buffered(1))

    return pl.pallas_call(
        beam_kernel,
        out_shape=(image, image),
        grid_spec=pltpu.PrefetchScalarGridSpec(
            num_scalar_prefetch=5,
            grid=(slots,),
            in_specs=[
                whole(rf.shape),
                whole((1, history)),
                pl.BlockSpec(
                    (None, 1, depth, voxels),
                    lambda i, side, offsets, fanout, live, owned: (
                        0, jnp.minimum(i, live[0] - 1), 0, 0,
                    ),
                ),
                whole(apod.shape),
            ],
            out_specs=[whole(image.shape), whole(image.shape)],
            scratch_shapes=[
                pltpu.VMEM((reach + LANES, window), jnp.float32),
                pltpu.VMEM((waves * reach, waves * window), jnp.bfloat16),
                pltpu.VMEM((waves, frames * elems, window), jnp.float32),
                pltpu.SMEM((tiles,), jnp.int32),
            ],
        ),
        compiler_params=pltpu.CompilerParams(
            dimension_semantics=("arbitrary",), vmem_limit_bytes=48 * 2**20
        ),
        name="beams",
    )(side, offsets, fanout, live, owned, rf, taps[None], weights, apod)


def on_device(
    rf_rows, filter_taps, interp_weights, apodization, fanout, live_slots, offsets, owned_tiles
):
    frames = rf_rows.shape[1]
    wave_groups = lax.axis_size("wave")
    side = lax.axis_index("section").astype(jnp.int32)[None]
    keep, send = local_images(
        side, rf_rows, filter_taps, interp_weights, apodization, fanout, live_slots, offsets,
        owned_tiles,
    )
    swap = [(0, 1), (1, 0)]
    pair = keep + lax.ppermute(send, "section", swap)
    parts = lax.all_to_all(pair, "tile", 0, 0, tiled=True)
    mine = jnp.sum(parts, axis=0)
    total = mine
    for hop in range(1, wave_groups):
        total = total + lax.ppermute(
            mine, "wave", [(i, (i + hop) % wave_groups) for i in range(wave_groups)]
        )
    power = jnp.sum(total * total, axis=0, keepdims=True) * (1.0 / frames)
    return power + lax.ppermute(power, "section", swap)


def solution(mesh):
    return jax.shard_map(
        on_device,
        mesh=mesh,
        in_specs=(
            P("wave", None, ("section", "tile"), None),
            P(),
            P(("section", "tile"), None, None, None),
            P("wave", None, None),
            P(("section", "tile"), None),
            P(("section", "tile")),
            P(("section", "tile"), None, "wave"),
            P(),
        ),
        out_specs=P("tile", None),
        check_vma=False,
    )
```

```python
import jax
import jax.numpy as jnp
from jax import lax
from jax.experimental import pallas as pl
from jax.experimental.pallas import tpu as pltpu
from jax.sharding import PartitionSpec as P

LANES = 128
SUBLANES = 8
STEP = 16


def beam_kernel(
    side, live, offsets_in, fanout_in, owned_in, rf_in, taps_in, weights_in, apod_in,
    keep, send,
    offsets, fanout, owned, place, taps, apod, rf, weights,
    table, shifted, filtered, other, small_sems, rf_sems, weight_sems,
):
    waves, frames, elems, samples = rf.shape
    slots, depth, voxels = weights.shape
    window = depth // elems
    history = taps.shape[1]
    reach = window + history + LANES
    half = frames // 2
    tiles = owned.shape[0]
    chunks = frames // STEP
    small = [
        pltpu.make_async_copy(source, target, small_sems.at[i])
        for i, (source, target) in enumerate(
            [
                (offsets_in, offsets), (fanout_in, fanout), (owned_in, owned),
                (taps_in, taps), (apod_in, apod),
            ]
        )
    ]

    def rf_copy(chunk):
        span = pl.ds(chunk * STEP, STEP)
        return pltpu.make_async_copy(rf_in.at[:, span], rf.at[:, span], rf_sems.at[chunk])

    def weight_copy(slot):
        return pltpu.make_async_copy(weights_in.at[0, slot], weights.at[slot], weight_sems.at[slot])

    for copy in small:
        copy.start()
    for chunk in range(chunks):
        rf_copy(chunk).start()
    count = live[0]
    pairs = (count + 1) // 2
    keep[...] = jnp.zeros_like(keep)
    send[...] = jnp.zeros_like(send)
    for copy in small:
        copy.wait()
    for slot in range(slots):

        @pl.when(slot < 2 * pairs)
        def _():
            weight_copy(slot).start()

    rows = reach + LANES
    line = jnp.concatenate(
        [
            jnp.zeros((1, window + history), jnp.float32),
            taps[...].astype(jnp.float32),
            jnp.zeros((1, rows - window - 2 * history), jnp.float32),
        ],
        axis=1,
    )
    spread = jnp.broadcast_to(line, (rows, rows))
    table[...] = pltpu.roll(spread, 0, 1, stride=1, stride_axis=0)[:, :window]

    def note(index, carry):
        place[owned[index]] = index
        return carry

    lax.fori_loop(0, tiles, note, 0)

    def aim(slot, turn):
        bases = []
        for wave in range(waves):
            start = offsets[0, wave, slot] - history
            base = jnp.minimum(start // LANES * LANES, samples - reach)
            shifted[turn, wave] = table[pl.ds(LANES - (start - base), reach), :].astype(
                jnp.bfloat16
            )
            bases.append(pl.multiple_of(base, LANES))
        return bases

    def fir(bases, first, target, turn):
        for wave in range(waves):
            cut = rf[wave, first : first + STEP, :, pl.ds(bases[wave], reach)].reshape(
                STEP * elems, reach
            )
            lines = jnp.dot(cut, shifted[turn, wave], preferred_element_type=jnp.float32).reshape(
                STEP, elems // SUBLANES, SUBLANES, window
            )
            for part in range(elems // SUBLANES):
                target[wave, part, first * SUBLANES : (first + STEP) * SUBLANES, :] = lines[
                    :, part
                ].reshape(STEP * SUBLANES, window)

    def interpolate(slot, elem, source):
        columns = []
        for each in (elem, elem + 1):
            lines = [
                source[
                    wave, each // SUBLANES, pl.ds(each % SUBLANES, frames, stride=SUBLANES), :
                ].astype(jnp.bfloat16)
                for wave in range(waves)
            ]
            columns.append(jnp.concatenate(lines, axis=0))
        return jnp.dot(
            jnp.concatenate(columns, axis=1),
            weights[slot, elem * window : (elem + 2) * window, :],
            preferred_element_type=jnp.float32,
        )

    def finish(slot, beam):
        voxel_tile = fanout[0, slot]
        term = jnp.zeros((frames, voxels), jnp.float32)
        for wave in range(waves):
            term += apod[wave, pl.ds(voxel_tile, 1), :] * beam[wave * frames : (wave + 1) * frames]
        term -= jnp.sum(term, axis=0, keepdims=True) * (1.0 / frames)
        where = place[voxel_tile]
        alive = slot < count
        swap = side[0] == 1
        keep[where] = jnp.where(alive, jnp.where(swap, term[half:], term[:half]), keep[where])
        send[where] = jnp.where(alive, jnp.where(swap, term[:half], term[half:]), send[where])

    def stage(slot, source, target, turn):
        bases = aim(jnp.minimum(slot + 1, slots - 1), turn)
        beam = jnp.zeros((waves * frames, voxels), jnp.float32)
        total = elems // 2
        done = 0
        for chunk in range(chunks):
            fir(bases, chunk * STEP, target, turn)
            goal = min(total, -(-total * (chunk + 1) // (chunks - 1)))
            for pair in range(done, goal):
                beam += interpolate(slot, pair * 2, source)
            if done < total and goal == total:
                finish(slot, beam)
            done = goal

    bases = aim(0, 1)
    for chunk in range(chunks):
        rf_copy(chunk).wait()
        fir(bases, chunk * STEP, filtered, 1)

    def two_slots(index, carry):
        weight_copy(2 * index).wait()
        weight_copy(2 * index + 1).wait()
        stage(2 * index, filtered, other, 0)
        stage(2 * index + 1, other, filtered, 1)
        return carry

    lax.fori_loop(0, pairs, two_slots, 0)


def local_images(side, rf, taps, weights, apod, fanout, live, offsets, owned, opts=()):
    waves, frames, elems, samples = rf.shape
    slots, depth, voxels = weights.shape[1:]
    window = depth // elems
    history = taps.shape[0]
    reach = window + history + LANES
    tiles = owned.shape[0]
    image = jax.ShapeDtypeStruct((tiles, frames // 2, voxels), jnp.float32)
    smem = pl.BlockSpec(memory_space=pltpu.SMEM)
    hbm = pl.BlockSpec(memory_space=pltpu.HBM)
    vmem = pl.BlockSpec(memory_space=pltpu.VMEM)
    lines = pltpu.VMEM((waves, elems // SUBLANES, frames * SUBLANES, window), jnp.float32)
    return pl.pallas_call(
        beam_kernel,
        out_shape=(image, image),
        in_specs=[smem, smem] + [hbm] * 7,
        out_specs=[vmem, vmem],
        scratch_shapes=[
            pltpu.SMEM((1, waves, slots), jnp.int32),
            pltpu.SMEM((1, slots), jnp.int32),
            pltpu.SMEM((tiles,), jnp.int32),
            pltpu.SMEM((tiles,), jnp.int32),
            pltpu.VMEM((1, history), jnp.bfloat16),
            pltpu.VMEM(apod.shape, jnp.float32),
            pltpu.VMEM(rf.shape, jnp.bfloat16),
            pltpu.VMEM(weights.shape[1:], jnp.bfloat16),
            pltpu.VMEM((reach + LANES, window), jnp.float32),
            pltpu.VMEM((2, waves, reach, window), jnp.bfloat16),
            lines,
            lines,
            pltpu.SemaphoreType.DMA((5,)),
            pltpu.SemaphoreType.DMA((frames // STEP,)),
            pltpu.SemaphoreType.DMA((slots,)),
        ],
        compiler_params=pltpu.CompilerParams(vmem_limit_bytes=48 * 2**20),
        name="beams",
    )(
        side,
        live,
        *[
            pltpu.with_memory_space_constraint(array, pltpu.HBM)
            for array in (
                offsets.transpose(0, 2, 1), fanout, owned, rf, taps[None], weights, apod,
            )
        ],
    )


def on_device(
    rf_rows, filter_taps, interp_weights, apodization, fanout, live_slots, offsets, owned_tiles
):
    frames = rf_rows.shape[1]
    wave_groups = lax.axis_size("wave")
    side = lax.axis_index("section").astype(jnp.int32)[None]
    keep, send = local_images(
        side, rf_rows, filter_taps, interp_weights, apodization, fanout, live_slots, offsets,
        owned_tiles,
    )
    swap = [(0, 1), (1, 0)]
    pair = keep + lax.ppermute(send, "section", swap)
    parts = lax.all_to_all(pair, "tile", 0, 0, tiled=True)
    mine = jnp.sum(parts, axis=0)
    total = mine
    for hop in range(1, wave_groups):
        total = total + lax.ppermute(
            mine, "wave", [(i, (i + hop) % wave_groups) for i in range(wave_groups)]
        )
    power = jnp.sum(total * total, axis=0, keepdims=True) * (1.0 / frames)
    return power + lax.ppermute(power, "section", swap)


def solution(mesh):
    return jax.shard_map(
        on_device,
        mesh=mesh,
        in_specs=(
            P("wave", None, ("section", "tile"), None),
            P(),
            P(("section", "tile"), None, None, None),
            P("wave", None, None),
            P(("section", "tile"), None),
            P(("section", "tile")),
            P(("section", "tile"), None, "wave"),
            P(),
        ),
        out_specs=P("tile", None),
        check_vma=False,
    )
```

```python
import jax
import jax.numpy as jnp
from jax import lax
from jax.experimental import pallas as pl
from jax.experimental.pallas import tpu as pltpu
from jax.sharding import PartitionSpec as P

LANES = 128
SUBLANES = 8
STEP = 16
ROWS = 4


def beam_kernel(
    side, row, live, offsets_in, fanout_in, owned_in, rf_in, taps_in, weights_in, apod_in,
    keep, send,
    offsets, fanout, owned, place, taps, apod, rf, weights,
    table, shifted, filtered, other, small_sems, rf_sems, weight_sems,
):
    waves, frames, elems, samples = rf.shape
    slots, depth, voxels = weights.shape
    window = depth // elems
    history = taps.shape[1]
    reach = window + history + LANES
    half = frames // 2
    tiles = owned.shape[0]
    chunks = frames // STEP
    small = [
        pltpu.make_async_copy(source, target, small_sems.at[i])
        for i, (source, target) in enumerate(
            [
                (offsets_in, offsets), (fanout_in, fanout), (owned_in, owned),
                (taps_in, taps), (apod_in, apod),
            ]
        )
    ]

    def rf_copy(chunk):
        span = pl.ds(chunk * STEP, STEP)
        return pltpu.make_async_copy(rf_in.at[:, span], rf.at[:, span], rf_sems.at[chunk])

    def weight_copy(slot):
        return pltpu.make_async_copy(weights_in.at[0, slot], weights.at[slot], weight_sems.at[slot])

    for copy in small:
        copy.start()
    for chunk in range(chunks):
        rf_copy(chunk).start()
    count = live[0]
    pairs = (count + 1) // 2
    keep[...] = jnp.zeros_like(keep)
    send[...] = jnp.zeros_like(send)
    for copy in small:
        copy.wait()
    for slot in range(slots):

        @pl.when(slot < 2 * pairs)
        def _():
            weight_copy(slot).start()

    rows = reach + LANES
    line = jnp.concatenate(
        [
            jnp.zeros((1, window + history), jnp.float32),
            taps[...].astype(jnp.float32),
            jnp.zeros((1, rows - window - 2 * history), jnp.float32),
        ],
        axis=1,
    )
    spread = jnp.broadcast_to(line, (rows, rows))
    table[...] = pltpu.roll(spread, 0, 1, stride=1, stride_axis=0)[:, :window]

    columns = tiles // ROWS

    def note(index, carry):
        ahead = lax.rem(index // columns - row[0] + ROWS, ROWS)
        place[owned[index]] = ahead * columns + lax.rem(index, columns)
        return carry

    lax.fori_loop(0, tiles, note, 0)

    def aim(slot, turn):
        bases = []
        for wave in range(waves):
            start = offsets[0, wave, slot] - history
            base = jnp.minimum(start // LANES * LANES, samples - reach)
            shifted[turn, wave] = table[pl.ds(LANES - (start - base), reach), :].astype(
                jnp.bfloat16
            )
            bases.append(pl.multiple_of(base, LANES))
        return bases

    def fir(bases, first, target, turn):
        for wave in range(waves):
            cut = rf[wave, first : first + STEP, :, pl.ds(bases[wave], reach)].reshape(
                STEP * elems, reach
            )
            lines = jnp.dot(cut, shifted[turn, wave], preferred_element_type=jnp.float32).reshape(
                STEP, elems // SUBLANES, SUBLANES, window
            )
            for part in range(elems // SUBLANES):
                target[wave, part, first * SUBLANES : (first + STEP) * SUBLANES, :] = lines[
                    :, part
                ].reshape(STEP * SUBLANES, window)

    def interpolate(slot, elem, source):
        columns = []
        for each in (elem, elem + 1):
            lines = [
                source[
                    wave, each // SUBLANES, pl.ds(each % SUBLANES, frames, stride=SUBLANES), :
                ].astype(jnp.bfloat16)
                for wave in range(waves)
            ]
            columns.append(jnp.concatenate(lines, axis=0))
        return jnp.dot(
            jnp.concatenate(columns, axis=1),
            weights[slot, elem * window : (elem + 2) * window, :],
            preferred_element_type=jnp.float32,
        )

    def finish(slot, beam):
        voxel_tile = fanout[0, slot]
        term = jnp.zeros((frames, voxels), jnp.float32)
        for wave in range(waves):
            term += apod[wave, pl.ds(voxel_tile, 1), :] * beam[wave * frames : (wave + 1) * frames]
        term -= jnp.sum(term, axis=0, keepdims=True) * (1.0 / frames)
        where = place[voxel_tile]
        alive = slot < count
        swap = side[0] == 1
        keep[where] = jnp.where(alive, jnp.where(swap, term[half:], term[:half]), keep[where])
        send[where] = jnp.where(alive, jnp.where(swap, term[:half], term[half:]), send[where])

    def stage(slot, source, target, turn):
        bases = aim(jnp.minimum(slot + 1, slots - 1), turn)
        beam = jnp.zeros((waves * frames, voxels), jnp.float32)
        total = elems // 2
        done = 0
        for chunk in range(chunks):
            fir(bases, chunk * STEP, target, turn)
            goal = min(total, -(-total * (chunk + 1) // (chunks - 1)))
            for pair in range(done, goal):
                beam += interpolate(slot, pair * 2, source)
            if done < total and goal == total:
                finish(slot, beam)
            done = goal

    bases = aim(0, 1)
    for chunk in range(chunks):
        rf_copy(chunk).wait()
        fir(bases, chunk * STEP, filtered, 1)

    def two_slots(index, carry):
        weight_copy(2 * index).wait()
        weight_copy(2 * index + 1).wait()
        stage(2 * index, filtered, other, 0)
        stage(2 * index + 1, other, filtered, 1)
        return carry

    lax.fori_loop(0, pairs, two_slots, 0)


def local_images(side, row, rf, taps, weights, apod, fanout, live, offsets, owned, opts=()):
    waves, frames, elems, samples = rf.shape
    slots, depth, voxels = weights.shape[1:]
    window = depth // elems
    history = taps.shape[0]
    reach = window + history + LANES
    tiles = owned.shape[0]
    image = jax.ShapeDtypeStruct((tiles, frames // 2, voxels), jnp.float32)
    smem = pl.BlockSpec(memory_space=pltpu.SMEM)
    hbm = pl.BlockSpec(memory_space=pltpu.HBM)
    vmem = pl.BlockSpec(memory_space=pltpu.VMEM)
    lines = pltpu.VMEM((waves, elems // SUBLANES, frames * SUBLANES, window), jnp.float32)
    return pl.pallas_call(
        beam_kernel,
        out_shape=(image, image),
        in_specs=[smem, smem, smem] + [hbm] * 7,
        out_specs=[vmem, vmem],
        scratch_shapes=[
            pltpu.SMEM((1, waves, slots), jnp.int32),
            pltpu.SMEM((1, slots), jnp.int32),
            pltpu.SMEM((tiles,), jnp.int32),
            pltpu.SMEM((tiles,), jnp.int32),
            pltpu.VMEM((1, history), jnp.bfloat16),
            pltpu.VMEM(apod.shape, jnp.float32),
            pltpu.VMEM(rf.shape, jnp.bfloat16),
            pltpu.VMEM(weights.shape[1:], jnp.bfloat16),
            pltpu.VMEM((reach + LANES, window), jnp.float32),
            pltpu.VMEM((2, waves, reach, window), jnp.bfloat16),
            lines,
            lines,
            pltpu.SemaphoreType.DMA((5,)),
            pltpu.SemaphoreType.DMA((frames // STEP,)),
            pltpu.SemaphoreType.DMA((slots,)),
        ],
        compiler_params=pltpu.CompilerParams(vmem_limit_bytes=48 * 2**20),
        name="beams",
    )(
        side,
        row,
        live,
        *[
            pltpu.with_memory_space_constraint(array, pltpu.HBM)
            for array in (
                offsets.transpose(0, 2, 1), fanout, owned, rf, taps[None], weights, apod,
            )
        ],
    )


def on_device(
    rf_rows, filter_taps, interp_weights, apodization, fanout, live_slots, offsets, owned_tiles
):
    frames = rf_rows.shape[1]
    wave_groups = lax.axis_size("wave")
    tiles = lax.axis_size("tile")
    columns = tiles // ROWS
    side = lax.axis_index("section").astype(jnp.int32)[None]
    row = lax.div(lax.axis_index("tile").astype(jnp.int32), jnp.int32(columns))[None]
    keep, send = local_images(
        side, row, rf_rows, filter_taps, interp_weights, apodization, fanout, live_slots, offsets,
        owned_tiles,
    )
    swap = [(0, 1), (1, 0)]
    got = lax.ppermute(send, "section", swap)
    pairs = [
        keep[at * columns : (at + 1) * columns] + got[at * columns : (at + 1) * columns]
        for at in range(ROWS)
    ]
    line = pairs[0]
    for hop in range(1, ROWS):
        line = line + lax.ppermute(
            pairs[hop], "tile", [(i, (i + hop * columns) % tiles) for i in range(tiles)]
        )
    groups = [[at * columns + i for i in range(columns)] for at in range(ROWS)]
    parts = lax.all_to_all(line, "tile", 0, 0, axis_index_groups=groups, tiled=True)
    mine = jnp.sum(parts, axis=0)
    total = mine
    for hop in range(1, wave_groups):
        total = total + lax.ppermute(
            mine, "wave", [(i, (i + hop) % wave_groups) for i in range(wave_groups)]
        )
    power = jnp.sum(total * total, axis=0, keepdims=True) * (1.0 / frames)
    return power + lax.ppermute(power, "section", swap)


def solution(mesh):
    return jax.shard_map(
        on_device,
        mesh=mesh,
        in_specs=(
            P("wave", None, ("section", "tile"), None),
            P(),
            P(("section", "tile"), None, None, None),
            P("wave", None, None),
            P(("section", "tile"), None),
            P(("section", "tile")),
            P(("section", "tile"), None, "wave"),
            P(),
        ),
        out_specs=P("tile", None),
        check_vma=False,
    )
```

```python
import jax
import jax.numpy as jnp
from jax import lax
from jax.experimental import pallas as pl
from jax.experimental.pallas import tpu as pltpu
from jax.sharding import PartitionSpec as P

LANES = 128
SUBLANES = 8
STEP = 16
ROWS = 4
BLOCK = 256
GROUP = 4


def beam_kernel(
    side, row, live, offsets_in, fanout_in, owned_in, rf_in, taps_in, weights_in, apod_in,
    keep, send,
    offsets, fanout, owned, place, taps, apod, rf, weights,
    toeplitz, filtered, small_sems, rf_sems, weight_sems,
):
    waves, frames, elems, samples = rf.shape
    slots, depth, voxels = weights.shape
    window = depth // elems
    history = taps.shape[1]
    half = frames // 2
    tiles = owned.shape[0]
    chunks = frames // STEP
    count = live[0]
    rounds = lax.div(count + GROUP - 1, GROUP)
    needed = rounds * GROUP
    small = [
        pltpu.make_async_copy(source, target, small_sems.at[i])
        for i, (source, target) in enumerate(
            [
                (offsets_in, offsets), (fanout_in, fanout), (owned_in, owned),
                (taps_in, taps), (apod_in, apod),
            ]
        )
    ]

    def rf_copy(unit):
        wave, chunk = lax.div(unit, chunks), lax.rem(unit, chunks)
        span = pl.ds(chunk * STEP, STEP)
        return pltpu.make_async_copy(
            rf_in.at[wave, span], rf.at[wave, span], rf_sems.at[unit]
        )

    def weight_copy(slot):
        return pltpu.make_async_copy(weights_in.at[0, slot], weights.at[slot], weight_sems.at[slot])

    for copy in small:
        copy.start()
    for unit in range(4):
        rf_copy(unit).start()
    keep[...] = jnp.zeros_like(keep)
    send[...] = jnp.zeros_like(send)
    for copy in small:
        copy.wait()
    width = 2 * BLOCK
    line = jnp.concatenate(
        [
            jnp.zeros((1, history), jnp.float32),
            taps[...].astype(jnp.float32),
            jnp.zeros((1, width - 2 * history), jnp.float32),
        ],
        axis=1,
    )
    flipped = jnp.concatenate([line[:, history:], line[:, :history]], axis=1)
    spread = jnp.broadcast_to(flipped, (BLOCK + history, width))
    toeplitz[...] = pltpu.roll(spread, width - history, 1, stride=1, stride_axis=0)[
        :, :BLOCK
    ].astype(jnp.bfloat16)

    columns = tiles // ROWS

    def note(index, carry):
        ahead = lax.rem(index // columns - row[0] + ROWS, ROWS)
        place[owned[index]] = ahead * columns + lax.rem(index, columns)
        return carry

    lax.fori_loop(0, tiles, note, 0)

    blocks = samples // BLOCK
    units = waves * chunks

    def spot(unit):
        wave, chunk = lax.div(unit, chunks), lax.rem(unit, chunks)
        return wave, pl.ds(pl.multiple_of(chunk * STEP, STEP), STEP)

    def filter_block(unit, block):
        wave, span = spot(unit)
        at = block * BLOCK
        back = min(at, history)
        cut = rf[wave, span, :, at - back : at + BLOCK].reshape(STEP * elems, back + BLOCK)
        lines = jnp.dot(
            cut, toeplitz[history - back :, :], preferred_element_type=jnp.float32
        ).astype(jnp.bfloat16)
        filtered[wave, :, span, at : at + BLOCK] = jnp.swapaxes(
            lines.reshape(STEP, elems, BLOCK), 0, 1
        )

    def two_units(index, carry):
        unit = 2 * index
        rf_copy(unit).wait()
        rf_copy(unit + 1).wait()
        for later in (unit + 4, unit + 5):

            @pl.when(later < units)
            def _():
                rf_copy(later).start()

        for slot in range(slots // 2):
            ahead = (index - units // 2 + 2) * (slots // 2) + slot

            @pl.when((ahead >= 0) & (ahead < needed))
            def _():
                weight_copy(ahead).start()

        for each in range(2):
            for block in range(blocks):
                filter_block(unit + each, block)
        return carry

    lax.fori_loop(0, units // 2, two_units, 0)

    lane_index = lax.broadcasted_iota(jnp.int32, (frames, LANES), 1)

    def do_slot(slot):
        cuts = []
        for wave in range(waves):
            start = offsets[0, wave, slot]
            tile = lax.div(start, LANES)
            shift = start - tile * LANES
            after = jnp.minimum(tile + 1, samples // LANES - 1)
            cuts.append(
                (
                    pl.multiple_of(tile * LANES, LANES),
                    pl.multiple_of(after * LANES, LANES),
                    lax.rem(LANES - shift, LANES),
                    lane_index >= shift,
                )
            )
        beam = jnp.zeros((waves * frames, voxels), jnp.float32)
        for elem in range(0, elems, 2):
            across = []
            for each in (elem, elem + 1):
                lines = []
                for wave, (tile, after, turn, inside) in enumerate(cuts):
                    joined = jnp.where(
                        inside,
                        filtered[wave, each, :, pl.ds(tile, LANES)],
                        filtered[wave, each, :, pl.ds(after, LANES)],
                    )
                    lines.append(pltpu.roll(joined, turn, 1))
                across.append(jnp.concatenate(lines, axis=0))
            beam += jnp.dot(
                jnp.concatenate(across, axis=1),
                weights[slot, elem * window : (elem + 2) * window, :],
                preferred_element_type=jnp.float32,
            )
        voxel_tile = fanout[0, slot]
        term = jnp.zeros((frames, voxels), jnp.float32)
        for wave in range(waves):
            term += apod[wave, pl.ds(voxel_tile, 1), :] * beam[wave * frames : (wave + 1) * frames]
        term -= jnp.sum(term, axis=0, keepdims=True) * (1.0 / frames)
        where = place[voxel_tile]
        alive = slot < count
        swap = side[0] == 1
        keep[where] = jnp.where(alive, jnp.where(swap, term[half:], term[:half]), keep[where])
        send[where] = jnp.where(alive, jnp.where(swap, term[:half], term[half:]), send[where])

    def some_slots(index, carry):
        for each in range(GROUP):
            weight_copy(GROUP * index + each).wait()
        for each in range(GROUP):
            do_slot(GROUP * index + each)
        return carry

    lax.fori_loop(0, rounds, some_slots, 0)


def local_images(side, row, rf, taps, weights, apod, fanout, live, offsets, owned, opts=()):
    waves, frames, elems, samples = rf.shape
    slots, depth, voxels = weights.shape[1:]
    history = taps.shape[0]
    tiles = owned.shape[0]
    image = jax.ShapeDtypeStruct((tiles, frames // 2, voxels), jnp.float32)
    smem = pl.BlockSpec(memory_space=pltpu.SMEM)
    hbm = pl.BlockSpec(memory_space=pltpu.HBM)
    vmem = pl.BlockSpec(memory_space=pltpu.VMEM)
    return pl.pallas_call(
        beam_kernel,
        out_shape=(image, image),
        in_specs=[smem, smem, smem] + [hbm] * 7,
        out_specs=[vmem, vmem],
        scratch_shapes=[
            pltpu.SMEM((1, waves, slots), jnp.int32),
            pltpu.SMEM((1, slots), jnp.int32),
            pltpu.SMEM((tiles,), jnp.int32),
            pltpu.SMEM((tiles,), jnp.int32),
            pltpu.VMEM((1, history), jnp.bfloat16),
            pltpu.VMEM(apod.shape, jnp.float32),
            pltpu.VMEM(rf.shape, jnp.bfloat16),
            pltpu.VMEM(weights.shape[1:], jnp.bfloat16),
            pltpu.VMEM((BLOCK + history, BLOCK), jnp.bfloat16),
            pltpu.VMEM((waves, elems, frames, samples), jnp.bfloat16),
            pltpu.SemaphoreType.DMA((5,)),
            pltpu.SemaphoreType.DMA((waves * (frames // STEP),)),
            pltpu.SemaphoreType.DMA((slots,)),
        ],
        compiler_params=pltpu.CompilerParams(vmem_limit_bytes=48 * 2**20),
        name="beams",
    )(
        side,
        row,
        live,
        *[
            pltpu.with_memory_space_constraint(array, pltpu.HBM)
            for array in (
                offsets.transpose(0, 2, 1), fanout, owned, rf, taps[None], weights, apod,
            )
        ],
    )


def on_device(
    rf_rows, filter_taps, interp_weights, apodization, fanout, live_slots, offsets, owned_tiles
):
    frames = rf_rows.shape[1]
    wave_groups = lax.axis_size("wave")
    tiles = lax.axis_size("tile")
    columns = tiles // ROWS
    side = lax.axis_index("section").astype(jnp.int32)[None]
    row = lax.div(lax.axis_index("tile").astype(jnp.int32), jnp.int32(columns))[None]
    keep, send = local_images(
        side, row, rf_rows, filter_taps, interp_weights, apodization, fanout, live_slots, offsets,
        owned_tiles,
    )
    swap = [(0, 1), (1, 0)]
    got = lax.ppermute(send, "section", swap)
    pairs = [
        keep[at * columns : (at + 1) * columns] + got[at * columns : (at + 1) * columns]
        for at in range(ROWS)
    ]
    line = pairs[0]
    for hop in range(1, ROWS):
        line = line + lax.ppermute(
            pairs[hop], "tile", [(i, (i + hop * columns) % tiles) for i in range(tiles)]
        )
    groups = [[at * columns + i for i in range(columns)] for at in range(ROWS)]
    parts = lax.all_to_all(line, "tile", 0, 0, axis_index_groups=groups, tiled=True)
    mine = jnp.sum(parts, axis=0)
    total = mine
    for hop in range(1, wave_groups):
        total = total + lax.ppermute(
            mine, "wave", [(i, (i + hop) % wave_groups) for i in range(wave_groups)]
        )
    power = jnp.sum(total * total, axis=0, keepdims=True) * (1.0 / frames)
    return power + lax.ppermute(power, "section", swap)


def solution(mesh):
    return jax.shard_map(
        on_device,
        mesh=mesh,
        in_specs=(
            P("wave", None, ("section", "tile"), None),
            P(),
            P(("section", "tile"), None, None, None),
            P("wave", None, None),
            P(("section", "tile"), None),
            P(("section", "tile")),
            P(("section", "tile"), None, "wave"),
            P(),
        ),
        out_specs=P("tile", None),
        check_vma=False,
    )
```

```python
import jax
import jax.numpy as jnp
from jax import lax
from jax.experimental import pallas as pl
from jax.experimental.pallas import tpu as pltpu
from jax.sharding import PartitionSpec as P

LANES = 128
SUBLANES = 8
STEP = 16
ROWS = 4
BLOCK = 256
GROUP = 4


def beam_kernel(
    side, row, live, offsets_in, fanout_in, owned_in, rf_in, taps_in, weights_in, apod_in,
    keep, send,
    offsets, fanout, owned, place, taps, apod, rf, weights,
    toeplitz, filtered, small_sems, rf_sems, weight_sems,
):
    waves, frames, elems, samples = rf.shape
    slots, depth, voxels = weights.shape
    window = depth // elems
    history = taps.shape[1]
    half = frames // 2
    tiles = owned.shape[0]
    chunks = frames // STEP
    count = live[0]
    rounds = lax.div(count + GROUP - 1, GROUP)
    needed = rounds * GROUP
    small = [
        pltpu.make_async_copy(source, target, small_sems.at[i])
        for i, (source, target) in enumerate(
            [
                (offsets_in, offsets), (fanout_in, fanout), (owned_in, owned),
                (taps_in, taps), (apod_in, apod),
            ]
        )
    ]

    def rf_copy(unit):
        wave, chunk = lax.div(unit, chunks), lax.rem(unit, chunks)
        span = pl.ds(chunk * STEP, STEP)
        return pltpu.make_async_copy(
            rf_in.at[wave, span], rf.at[wave, span], rf_sems.at[unit]
        )

    def weight_copy(slot):
        return pltpu.make_async_copy(weights_in.at[0, slot], weights.at[slot], weight_sems.at[slot])

    for copy in small:
        copy.start()
    for unit in range(2):
        rf_copy(unit).start()
    keep[...] = jnp.zeros_like(keep)
    send[...] = jnp.zeros_like(send)
    for copy in small:
        copy.wait()
    width = 2 * BLOCK
    line = jnp.concatenate(
        [
            jnp.zeros((1, history), jnp.float32),
            taps[...].astype(jnp.float32),
            jnp.zeros((1, width - 2 * history), jnp.float32),
        ],
        axis=1,
    )
    flipped = jnp.concatenate([line[:, history:], line[:, :history]], axis=1)
    spread = jnp.broadcast_to(flipped, (BLOCK + history, width))
    toeplitz[...] = pltpu.roll(spread, width - history, 1, stride=1, stride_axis=0)[
        :, :BLOCK
    ].astype(jnp.bfloat16)

    columns = tiles // ROWS

    def note(index, carry):
        ahead = lax.rem(index // columns - row[0] + ROWS, ROWS)
        place[owned[index]] = ahead * columns + lax.rem(index, columns)
        return carry

    lax.fori_loop(0, tiles, note, 0)

    blocks = samples // BLOCK
    units = waves * chunks

    def spot(unit):
        wave, chunk = lax.div(unit, chunks), lax.rem(unit, chunks)
        return wave, pl.ds(pl.multiple_of(chunk * STEP, STEP), STEP)

    def filter_block(unit, block):
        wave, span = spot(unit)
        at = block * BLOCK
        back = min(at, history)
        cut = rf[wave, span, :, at - back : at + BLOCK].reshape(STEP * elems, back + BLOCK)
        lines = jnp.dot(
            cut, toeplitz[history - back :, :], preferred_element_type=jnp.float32
        ).astype(jnp.bfloat16)
        filtered[wave, :, span, at : at + BLOCK] = jnp.swapaxes(
            lines.reshape(STEP, elems, BLOCK), 0, 1
        )

    def two_units(index, carry):
        unit = 2 * index
        rf_copy(unit).wait()
        rf_copy(unit + 1).wait()
        for later in (unit + 4, unit + 5):

            @pl.when(later < units)
            def _():
                rf_copy(later).start()

        for slot in range(slots // 2):
            ahead = (index - units // 2 + 2) * (slots // 2) + slot

            @pl.when((ahead >= 0) & (ahead < needed))
            def _():
                weight_copy(ahead).start()

        for each in range(2):
            for block in range(blocks):
                filter_block(unit + each, block)
        return carry

    for unit in range(2, 4):
        rf_copy(unit).start()
    lax.fori_loop(0, units // 2, two_units, 0)

    lane_index = lax.broadcasted_iota(jnp.int32, (frames, LANES), 1)

    def do_slot(slot):
        cuts = []
        for wave in range(waves):
            start = offsets[0, wave, slot]
            tile = lax.div(start, LANES)
            shift = start - tile * LANES
            after = jnp.minimum(tile + 1, samples // LANES - 1)
            cuts.append(
                (
                    pl.multiple_of(tile * LANES, LANES),
                    pl.multiple_of(after * LANES, LANES),
                    lax.rem(LANES - shift, LANES),
                    lane_index >= shift,
                )
            )
        beam = jnp.zeros((waves * frames, voxels), jnp.float32)
        for elem in range(0, elems, 2):
            across = []
            for each in (elem, elem + 1):
                lines = []
                for wave, (tile, after, turn, inside) in enumerate(cuts):
                    joined = jnp.where(
                        inside,
                        filtered[wave, each, :, pl.ds(tile, LANES)],
                        filtered[wave, each, :, pl.ds(after, LANES)],
                    )
                    lines.append(pltpu.roll(joined, turn, 1))
                across.append(jnp.concatenate(lines, axis=0))
            beam += jnp.dot(
                jnp.concatenate(across, axis=1),
                weights[slot, elem * window : (elem + 2) * window, :],
                preferred_element_type=jnp.float32,
            )
        voxel_tile = fanout[0, slot]
        term = jnp.zeros((frames, voxels), jnp.float32)
        for wave in range(waves):
            term += apod[wave, pl.ds(voxel_tile, 1), :] * beam[wave * frames : (wave + 1) * frames]
        term -= jnp.sum(term, axis=0, keepdims=True) * (1.0 / frames)
        where = place[voxel_tile]
        alive = slot < count
        swap = side[0] == 1
        keep[where] = jnp.where(alive, jnp.where(swap, term[half:], term[:half]), keep[where])
        send[where] = jnp.where(alive, jnp.where(swap, term[:half], term[half:]), send[where])

    def some_slots(index, carry):
        for each in range(GROUP):
            weight_copy(GROUP * index + each).wait()
        for each in range(GROUP):
            do_slot(GROUP * index + each)
        return carry

    lax.fori_loop(0, rounds, some_slots, 0)


def local_images(side, row, rf, taps, weights, apod, fanout, live, offsets, owned):
    waves, frames, elems, samples = rf.shape
    slots, depth, voxels = weights.shape[1:]
    history = taps.shape[0]
    tiles = owned.shape[0]
    image = jax.ShapeDtypeStruct((tiles, frames // 2, voxels), jnp.float32)
    smem = pl.BlockSpec(memory_space=pltpu.SMEM)
    hbm = pl.BlockSpec(memory_space=pltpu.HBM)
    vmem = pl.BlockSpec(memory_space=pltpu.VMEM)
    return pl.pallas_call(
        beam_kernel,
        out_shape=(image, image),
        in_specs=[smem, smem, smem] + [hbm] * 7,
        out_specs=[vmem, vmem],
        scratch_shapes=[
            pltpu.SMEM((1, waves, slots), jnp.int32),
            pltpu.SMEM((1, slots), jnp.int32),
            pltpu.SMEM((tiles,), jnp.int32),
            pltpu.SMEM((tiles,), jnp.int32),
            pltpu.VMEM((1, history), jnp.bfloat16),
            pltpu.VMEM(apod.shape, jnp.float32),
            pltpu.VMEM(rf.shape, jnp.bfloat16),
            pltpu.VMEM(weights.shape[1:], jnp.bfloat16),
            pltpu.VMEM((BLOCK + history, BLOCK), jnp.bfloat16),
            pltpu.VMEM((waves, elems, frames, samples), jnp.bfloat16),
            pltpu.SemaphoreType.DMA((5,)),
            pltpu.SemaphoreType.DMA((waves * (frames // STEP),)),
            pltpu.SemaphoreType.DMA((slots,)),
        ],
        compiler_params=pltpu.CompilerParams(vmem_limit_bytes=48 * 2**20),
        name="beams",
    )(
        side,
        row,
        live,
        *[
            pltpu.with_memory_space_constraint(array, pltpu.HBM)
            for array in (
                offsets.transpose(0, 2, 1), fanout, owned, rf, taps[None], weights, apod,
            )
        ],
    )


def on_device(
    rf_rows, filter_taps, interp_weights, apodization, fanout, live_slots, offsets, owned_tiles
):
    frames = rf_rows.shape[1]
    wave_groups = lax.axis_size("wave")
    tiles = lax.axis_size("tile")
    columns = tiles // ROWS
    side = lax.axis_index("section").astype(jnp.int32)[None]
    row = lax.div(lax.axis_index("tile").astype(jnp.int32), jnp.int32(columns))[None]
    keep, send = local_images(
        side, row, rf_rows, filter_taps, interp_weights, apodization, fanout, live_slots, offsets,
        owned_tiles,
    )
    swap = [(0, 1), (1, 0)]
    got = lax.ppermute(send, "section", swap)
    pairs = [
        keep[at * columns : (at + 1) * columns] + got[at * columns : (at + 1) * columns]
        for at in range(ROWS)
    ]
    line = pairs[0]
    for hop in range(1, ROWS):
        line = line + lax.ppermute(
            pairs[hop], "tile", [(i, (i + hop * columns) % tiles) for i in range(tiles)]
        )
    groups = [[at * columns + i for i in range(columns)] for at in range(ROWS)]
    parts = lax.all_to_all(line, "tile", 0, 0, axis_index_groups=groups, tiled=True)
    mine = jnp.sum(parts, axis=0)
    total = mine
    for hop in range(1, wave_groups):
        total = total + lax.ppermute(
            mine, "wave", [(i, (i + hop) % wave_groups) for i in range(wave_groups)]
        )
    power = jnp.sum(total * total, axis=0, keepdims=True) * (1.0 / frames)
    return power + lax.ppermute(power, "section", swap)


def solution(mesh):
    return jax.shard_map(
        on_device,
        mesh=mesh,
        in_specs=(
            P("wave", None, ("section", "tile"), None),
            P(),
            P(("section", "tile"), None, None, None),
            P("wave", None, None),
            P(("section", "tile"), None),
            P(("section", "tile")),
            P(("section", "tile"), None, "wave"),
            P(),
        ),
        out_specs=P("tile", None),
        check_vma=False,
    )
```

```python
import jax
import jax.numpy as jnp
from jax import lax
from jax.experimental import pallas as pl
from jax.experimental.pallas import tpu as pltpu
from jax.sharding import PartitionSpec as P

LANES = 128
SUBLANES = 8
STEP = 16
ROWS = 4
BLOCK = 256
GROUP = 4


def beam_kernel(
    side, row, live, offsets_in, fanout_in, owned_in, rf_in, taps_in, weights_in, apod_in,
    keep, send,
    offsets, fanout, owned, place, taps, apod, rf, weights,
    toeplitz, filtered, small_sems, rf_sems, weight_sems,
):
    waves, frames, elems, samples = rf.shape
    slots, depth, voxels = weights.shape
    window = depth // elems
    history = taps.shape[1]
    half = frames // 2
    tiles = owned.shape[0]
    chunks = frames // STEP
    count = live[0]
    rounds = lax.div(count + GROUP - 1, GROUP)
    needed = rounds * GROUP
    small = [
        pltpu.make_async_copy(source, target, small_sems.at[i])
        for i, (source, target) in enumerate(
            [
                (offsets_in, offsets), (fanout_in, fanout), (owned_in, owned),
                (taps_in, taps), (apod_in, apod),
            ]
        )
    ]

    def rf_copy(unit):
        wave, chunk = lax.div(unit, chunks), lax.rem(unit, chunks)
        span = pl.ds(chunk * STEP, STEP)
        return pltpu.make_async_copy(
            rf_in.at[wave, span], rf.at[wave, span], rf_sems.at[unit]
        )

    def weight_copy(slot):
        return pltpu.make_async_copy(weights_in.at[0, slot], weights.at[slot], weight_sems.at[slot])

    for copy in small:
        copy.start()
    for unit in range(2):
        rf_copy(unit).start()
    keep[...] = jnp.zeros_like(keep)
    send[...] = jnp.zeros_like(send)
    small[3].wait()
    width = 2 * BLOCK
    line = jnp.concatenate(
        [
            jnp.zeros((1, history), jnp.float32),
            taps[...].astype(jnp.float32),
            jnp.zeros((1, width - 2 * history), jnp.float32),
        ],
        axis=1,
    )
    flipped = jnp.concatenate([line[:, history:], line[:, :history]], axis=1)
    spread = jnp.broadcast_to(flipped, (BLOCK + history, width))
    toeplitz[...] = pltpu.roll(spread, width - history, 1, stride=1, stride_axis=0)[
        :, :BLOCK
    ].astype(jnp.bfloat16)


    blocks = samples // BLOCK
    units = waves * chunks

    def spot(unit):
        wave, chunk = lax.div(unit, chunks), lax.rem(unit, chunks)
        return wave, pl.ds(pl.multiple_of(chunk * STEP, STEP), STEP)

    def filter_block(unit, block):
        wave, span = spot(unit)
        at = block * BLOCK
        back = min(at, history)
        cut = rf[wave, span, :, at - back : at + BLOCK].reshape(STEP * elems, back + BLOCK)
        lines = jnp.dot(
            cut, toeplitz[history - back :, :], preferred_element_type=jnp.float32
        ).astype(jnp.bfloat16)
        filtered[wave, :, span, at : at + BLOCK] = jnp.swapaxes(
            lines.reshape(STEP, elems, BLOCK), 0, 1
        )

    def two_units(index, carry):
        unit = 2 * index
        rf_copy(unit).wait()
        rf_copy(unit + 1).wait()
        for later in (unit + 4, unit + 5):

            @pl.when(later < units)
            def _():
                rf_copy(later).start()

        for slot in range(slots // 2):
            ahead = (index - units // 2 + 2) * (slots // 2) + slot

            @pl.when((ahead >= 0) & (ahead < needed))
            def _():
                weight_copy(ahead).start()

        for each in range(2):
            for block in range(blocks):
                filter_block(unit + each, block)
        return carry

    for unit in range(2, 4):
        rf_copy(unit).start()
    lax.fori_loop(0, units // 2, two_units, 0)

    for at in (0, 1, 2, 4):
        small[at].wait()
    columns = tiles // ROWS
    for line_of in range(ROWS):
        ahead = lax.rem(line_of + ROWS - row[0], ROWS) * columns
        for index in range(columns):
            place[owned[line_of * columns + index]] = ahead + index

    lane_index = lax.broadcasted_iota(jnp.int32, (frames, LANES), 1)

    def do_slot(slot):
        cuts = []
        for wave in range(waves):
            start = offsets[0, wave, slot]
            tile = lax.div(start, LANES)
            shift = start - tile * LANES
            after = jnp.minimum(tile + 1, samples // LANES - 1)
            cuts.append(
                (
                    pl.multiple_of(tile * LANES, LANES),
                    pl.multiple_of(after * LANES, LANES),
                    lax.rem(LANES - shift, LANES),
                    lane_index >= shift,
                )
            )
        beam = jnp.zeros((waves * frames, voxels), jnp.float32)
        for elem in range(0, elems, 2):
            across = []
            for each in (elem, elem + 1):
                lines = []
                for wave, (tile, after, turn, inside) in enumerate(cuts):
                    joined = jnp.where(
                        inside,
                        filtered[wave, each, :, pl.ds(tile, LANES)],
                        filtered[wave, each, :, pl.ds(after, LANES)],
                    )
                    lines.append(pltpu.roll(joined, turn, 1))
                across.append(jnp.concatenate(lines, axis=0))
            beam += jnp.dot(
                jnp.concatenate(across, axis=1),
                weights[slot, elem * window : (elem + 2) * window, :],
                preferred_element_type=jnp.float32,
            )
        voxel_tile = fanout[0, slot]
        term = jnp.zeros((frames, voxels), jnp.float32)
        for wave in range(waves):
            term += apod[wave, pl.ds(voxel_tile, 1), :] * beam[wave * frames : (wave + 1) * frames]
        term -= jnp.sum(term, axis=0, keepdims=True) * (1.0 / frames)
        where = place[voxel_tile]
        alive = slot < count
        swap = side[0] == 1
        keep[where] = jnp.where(alive, jnp.where(swap, term[half:], term[:half]), keep[where])
        send[where] = jnp.where(alive, jnp.where(swap, term[:half], term[half:]), send[where])

    def some_slots(index, carry):
        for each in range(GROUP):
            weight_copy(GROUP * index + each).wait()
        for each in range(GROUP):
            do_slot(GROUP * index + each)
        return carry

    lax.fori_loop(0, rounds, some_slots, 0)


def local_images(side, row, rf, taps, weights, apod, fanout, live, offsets, owned):
    waves, frames, elems, samples = rf.shape
    slots, depth, voxels = weights.shape[1:]
    history = taps.shape[0]
    tiles = owned.shape[0]
    image = jax.ShapeDtypeStruct((tiles, frames // 2, voxels), jnp.float32)
    smem = pl.BlockSpec(memory_space=pltpu.SMEM)
    hbm = pl.BlockSpec(memory_space=pltpu.HBM)
    vmem = pl.BlockSpec(memory_space=pltpu.VMEM)
    return pl.pallas_call(
        beam_kernel,
        out_shape=(image, image),
        in_specs=[smem, smem, smem] + [hbm] * 7,
        out_specs=[vmem, vmem],
        scratch_shapes=[
            pltpu.SMEM((1, waves, slots), jnp.int32),
            pltpu.SMEM((1, slots), jnp.int32),
            pltpu.SMEM((tiles,), jnp.int32),
            pltpu.SMEM((tiles,), jnp.int32),
            pltpu.VMEM((1, history), jnp.bfloat16),
            pltpu.VMEM(apod.shape, jnp.float32),
            pltpu.VMEM(rf.shape, jnp.bfloat16),
            pltpu.VMEM(weights.shape[1:], jnp.bfloat16),
            pltpu.VMEM((BLOCK + history, BLOCK), jnp.bfloat16),
            pltpu.VMEM((waves, elems, frames, samples), jnp.bfloat16),
            pltpu.SemaphoreType.DMA((5,)),
            pltpu.SemaphoreType.DMA((waves * (frames // STEP),)),
            pltpu.SemaphoreType.DMA((slots,)),
        ],
        compiler_params=pltpu.CompilerParams(vmem_limit_bytes=48 * 2**20),
        name="beams",
    )(
        side,
        row,
        live,
        *[
            pltpu.with_memory_space_constraint(array, pltpu.HBM)
            for array in (
                offsets.transpose(0, 2, 1), fanout, owned, rf, taps[None], weights, apod,
            )
        ],
    )


def on_device(
    rf_rows, filter_taps, interp_weights, apodization, fanout, live_slots, offsets, owned_tiles
):
    frames = rf_rows.shape[1]
    wave_groups = lax.axis_size("wave")
    tiles = lax.axis_size("tile")
    columns = tiles // ROWS
    side = lax.axis_index("section").astype(jnp.int32)[None]
    row = lax.div(lax.axis_index("tile").astype(jnp.int32), jnp.int32(columns))[None]
    keep, send = local_images(
        side, row, rf_rows, filter_taps, interp_weights, apodization, fanout, live_slots, offsets,
        owned_tiles,
    )
    swap = [(0, 1), (1, 0)]
    got = lax.ppermute(send, "section", swap)
    pairs = [
        keep[at * columns : (at + 1) * columns] + got[at * columns : (at + 1) * columns]
        for at in range(ROWS)
    ]
    line = pairs[0]
    for hop in range(1, ROWS):
        line = line + lax.ppermute(
            pairs[hop], "tile", [(i, (i + hop * columns) % tiles) for i in range(tiles)]
        )
    groups = [[at * columns + i for i in range(columns)] for at in range(ROWS)]
    parts = lax.all_to_all(line, "tile", 0, 0, axis_index_groups=groups, tiled=True)
    mine = jnp.sum(parts, axis=0)
    total = mine
    for hop in range(1, wave_groups):
        total = total + lax.ppermute(
            mine, "wave", [(i, (i + hop) % wave_groups) for i in range(wave_groups)]
        )
    power = jnp.sum(total * total, axis=0, keepdims=True) * (1.0 / frames)
    return power + lax.ppermute(power, "section", swap)


def solution(mesh):
    return jax.shard_map(
        on_device,
        mesh=mesh,
        in_specs=(
            P("wave", None, ("section", "tile"), None),
            P(),
            P(("section", "tile"), None, None, None),
            P("wave", None, None),
            P(("section", "tile"), None),
            P(("section", "tile")),
            P(("section", "tile"), None, "wave"),
            P(),
        ),
        out_specs=P("tile", None),
        check_vma=False,
    )
```
